512 devices in a mesh: dom: 4 (over x), tp: 32 (over z_hi, y, core), dp: 4 (over z_lo).
Axes of the slice: x: 4, y: 8, z: 8 (z_hi: 2, z_lo: 4; z = z_hi * 4 + z_lo), core: 2. Of those that a mesh axis runs over, the one named last changes fastest.
Arguments:
- query: bfloat16 [32, 16, 8192], P('tp'), may hold values from -12 to 12
- key_block_pool: bfloat16 [32, 8192, 1024], P('tp', ('dom', 'dp')), may hold values from -6 to 6
- value_block_pool: bfloat16 [32, 8192, 1024], P('tp', ('dom', 'dp')), may hold values from -12 to 12
- row_blocks: int32 [32, 16], P('tp'), may hold values from 1 to 32, 64 in all within a row
- trim: int32 [32, 16], P('tp'), may hold values from 0 to 127
- ffn_in: bfloat16 [256, 8192], P('tp', ('dom', 'dp')), may hold values from -6 to 6
- w_gate: bfloat16 [8192, 28672], P(('dom', 'dp'), 'tp'), may hold values from -0.0625 to 0.0625
- w_up: bfloat16 [8192, 28672], P(('dom', 'dp'), 'tp'), may hold values from -0.0625 to 0.0625
- w_down: bfloat16 [28672, 8192], P('tp', ('dom', 'dp')), may hold values from -0.03125 to 0.03125
Outputs:
- attn_out: bfloat16 [32, 16, 8192], P('tp', None, ('dom', 'dp'))
- ffn_out: bfloat16 [256, 8192], P('tp', ('dom', 'dp'))
The draws below stay inside these ranges and needn't reach their ends.
Inputs may be any that keep to these rules, and one draw needn't show every extreme that they name: `row_blocks`: each attention row holds 1 to 32 blocks; the 16 rows of one row group (one line of the array) together fill its pool of 64 blocks exactly, and some row holds 32 blocks.
All inputs are finite; a program needn't handle non-finite values.
Results may differ from the reference program's by a relative error of at most 0.006.
Values may be sent and summed in bfloat16 or wider, within the bound.
A program may use at most 64 MiB of HBM per device.

```python
import math
import jax
import jax.numpy as jnp
import numpy as np
from jax import lax

D = 8192
FF = 28672
QUERY_HEADS = 64
KEY_HEADS = 8
HEAD_SIZE = 128
BLOCK_POSITIONS = 128
MOST_BLK = 32
BLK_DEV = 4
RG = 16
GROUP_BLOCKS = 64
ROWS_F = 256
N_DOM = 4
N_TP = 32
N_DP = 4


def draw_query(key, part):
    key = jax.random.fold_in(key, 11)
    first = jax.random.fold_in(key, 0)
    random_jitter = jax.random.normal(first, (N_TP, RG, QUERY_HEADS, HEAD_SIZE), jnp.float32)
    values = jnp.clip(2.0 * random_jitter, -12.0, 12.0)
    return values.reshape(N_TP, RG, QUERY_HEADS * HEAD_SIZE).astype(jnp.bfloat16)


def draw_key_block_pool(key, part):
    key = jax.random.fold_in(key, 23)
    cache_cells = BLK_DEV * N_DOM * N_DP * BLOCK_POSITIONS
    random_jitter = jnp.clip(jax.random.normal(key, (N_TP, cache_cells, KEY_HEADS * HEAD_SIZE), jnp.float32), -6.0, 6.0)
    values = random_jitter
    return values.astype(jnp.bfloat16)


def set_ends(result, own_key, smallest, high):
    spot = [jax.random.randint(jax.random.fold_in(own_key, axis), (), 0, length) for axis, length in enumerate(result.shape)]
    main_axis = result.shape.index(max(result.shape))
    beside = spot[:main_axis] + [(spot[main_axis] + 1) % result.shape[main_axis]] + spot[main_axis + 1:]
    return result.at[tuple(spot)].set(smallest).at[tuple(beside)].set(high)


def level_of(stream_key, shape, pieces, least, high):
    loudness, own = 1.0, jax.random.fold_in(stream_key, 6)
    for position, parts in pieces:
        steps = jnp.exp(jax.random.uniform(jax.random.fold_in(own, position), (parts,), jnp.float32, least / len(pieces), high / len(pieces)))
        loudness = loudness * jnp.repeat(steps, shape[position] // parts).reshape([-1 if axis == position else 1 for axis in range(len(shape))])
    return loudness


def profile(count, total, limit, lean):
    weights = [(1 << 20) // math.isqrt(grade ** lean) + 1 for grade in range(2, count + 1)]
    spare, given = total - limit - (count - 1), [1] * (count - 1)
    while spare > 0:
        movable = [i for i in range(count - 1) if given[i] < limit]
        mass, budget = sum([weights[i] for i in movable]), spare
        for i in movable:
            addition = min(limit - given[i], max(1, budget * weights[i] // mass), spare)
            given[i] = given[i] + addition
            spare = spare - addition
    return np.array([limit] + given)


def ragged(key, count, total, bound, lean):
    if count == 2:
        one = jax.random.randint(key, (), max(1, total - bound), min(bound, total - 1) + 1)
        return jnp.stack([one, total - one])
    tallies = jnp.asarray(profile(count, total, bound, lean), jnp.int32)
    couples = (count - 1) // 2
    donor, taker = tallies[1:1 + 2 * couples:2], tallies[2:2 + 2 * couples:2]
    slack = jnp.minimum(donor - 1, bound - taker)
    moved = jax.random.randint(jax.random.fold_in(key, 1), (couples,), 0, 1 << 20) % (slack + 1)
    tallies = tallies.at[1:1 + 2 * couples:2].set(donor - moved).at[2:2 + 2 * couples:2].set(taker + moved)
    return tallies[jax.random.permutation(jax.random.fold_in(key, 2), count)]


def bell_draw(own_key, extent, scale, bound, cuts=(), held_as=jnp.bfloat16):
    loudness = level_of(own_key, extent, cuts, -0.22, 0.18) if cuts else 1.0
    result = jax.random.normal(own_key, extent, jnp.float32) * scale * loudness
    return jnp.minimum(jnp.maximum(result, -bound), bound).astype(held_as)


def setup_inputs(seed: int = 0) -> dict:
    streams_of = jax.random.split(jax.random.key(seed), 10)
    return {
        "query": draw_query(jax.random.fold_in(streams_of[9], 71), 0),
        "key_block_pool": draw_key_block_pool(jax.random.fold_in(streams_of[9], 71), 0),
        "value_block_pool": bell_draw(streams_of[2], (N_TP, GROUP_BLOCKS * BLOCK_POSITIONS, KEY_HEADS * HEAD_SIZE), 2.0, 12.0, ((0, 32), (1, 16))),
        "row_blocks": jax.vmap(lambda own: ragged(own, RG, GROUP_BLOCKS, MOST_BLK, 2))(jax.random.split(streams_of[3], N_TP)).reshape((N_TP, RG)).astype(jnp.int32),
        "trim": set_ends(jax.random.randint(streams_of[4], (N_TP, RG), 0, BLOCK_POSITIONS), jax.random.fold_in(streams_of[4], 1), 0, BLOCK_POSITIONS - 1).astype(jnp.int32),
        "ffn_in": bell_draw(streams_of[5], (ROWS_F, D), 1.0, 6.0, ((0, 32), (1, 16))),
        "w_gate": bell_draw(streams_of[6], (D, FF), D ** -0.5, 0.0625, ((0, 16), (1, 32))),
        "w_up": bell_draw(streams_of[7], (D, FF), D ** -0.5, 0.0625, ((0, 16), (1, 32))),
        "w_down": bell_draw(streams_of[8], (FF, D), FF ** -0.5, 0.03125, ((0, 32), (1, 16))),
    }


NEG = -1e30


def group_attention(args):
    group_query, group_keys, group_values, counts, trims = args
    block_count = group_keys.shape[0] // BLOCK_POSITIONS
    row_group = QUERY_HEADS // KEY_HEADS
    starts = jnp.cumsum(counts) - counts
    index = jnp.arange(block_count, dtype=jnp.int32)
    block_row_index = (jnp.sum((starts[None, :] <= index[:, None]).astype(jnp.int32), axis=1) - 1).astype(jnp.int32)
    inner = index - starts[block_row_index]
    last = inner == counts[block_row_index] - 1
    cache_cells = jnp.arange(BLOCK_POSITIONS, dtype=jnp.int32)
    live = jnp.logical_or(jnp.logical_not(last)[:, None], cache_cells[None, :] < (BLOCK_POSITIONS - trims[block_row_index])[:, None])
    query_block = group_query[block_row_index].astype(jnp.float32).reshape(block_count, KEY_HEADS, row_group, HEAD_SIZE)
    key_block = group_keys.astype(jnp.float32).reshape(block_count, BLOCK_POSITIONS, KEY_HEADS, HEAD_SIZE)
    value_block = group_values.astype(jnp.float32).reshape(block_count, BLOCK_POSITIONS, KEY_HEADS, HEAD_SIZE)
    scores = jnp.einsum('bkgd,btkd->bkgt', query_block, key_block) * (HEAD_SIZE ** -0.5)
    scores = jnp.where(live[:, None, None, :], scores, NEG)
    onehot = block_row_index[:, None] == jnp.arange(RG, dtype=jnp.int32)[None, :]
    bmax = jnp.max(scores, axis=3)
    top = jnp.max(jnp.where(onehot[:, :, None, None], bmax[:, None], NEG), axis=0)
    weights = jnp.exp(scores - top[block_row_index][..., None]).astype(jnp.bfloat16).astype(jnp.float32)
    den_b = jnp.sum(weights, axis=3)
    num_b = jnp.einsum('bkgt,btkd->bkgd', weights, value_block)
    sel = onehot.astype(jnp.float32)
    numer = jnp.einsum('br,bx->rx', sel, num_b.reshape(block_count, QUERY_HEADS * HEAD_SIZE))
    total = jnp.einsum('br,bx->rx', sel, den_b.reshape(block_count, QUERY_HEADS))
    out = numer.reshape(RG, QUERY_HEADS, HEAD_SIZE) / total[..., None]
    return out.reshape(RG, QUERY_HEADS * HEAD_SIZE).astype(jnp.bfloat16)


def reference(query, key_block_pool, value_block_pool, row_blocks, trim, ffn_in, w_gate, w_up, w_down):
    attn_out = lax.map(group_attention, (query, key_block_pool, value_block_pool, row_blocks, trim))
    gate = jnp.dot(ffn_in, w_gate, preferred_element_type=jnp.float32)
    up = jnp.dot(ffn_in, w_up, preferred_element_type=jnp.float32)
    hidden = (jax.nn.silu(gate) * up).astype(jnp.bfloat16)
    ffn_out = jnp.dot(hidden, w_down, preferred_element_type=jnp.float32).astype(jnp.bfloat16)
    return attn_out, ffn_out
```

```python
import jax
import jax.numpy as jnp
from jax import lax
from jax.experimental import pallas as pl
from jax.experimental.pallas import tpu as pltpu
from jax.sharding import PartitionSpec as P

QUERY_HEADS = 64
KEY_HEADS = 8
HEAD_SIZE = 128
NEG = -1e30
MESH = pl.DeviceIdType.MESH
F32 = jnp.float32
BF16 = jnp.bfloat16

PLANE = [(i, j) for i in range(4) for j in range(4) if i or j]
CHIPS = [(i, j) for i in range(2) for j in range(8) if i or j]


def iota(shape, axis):
    return lax.broadcasted_iota(jnp.int32, shape, axis)


def fold(rows):
    return jnp.concatenate([rows[:, :256], rows[:, 256:]], axis=0)


def unfold(piece):
    return jnp.concatenate([piece[:8], piece[8:]], axis=1)


def kernel(
    q_hbm, k_hbm, v_hbm, count_ref, trim_ref, rows_ref, wg_hbm, wu_hbm, wd_hbm,
    attn_ref, ffn_ref,
    q, k, v, wg, wu, wd,
    xp, xmat, psend, xr, zsend, zr, hall, ysend, yr, fsend, fr, asend, ar,
    load_sem, x_s, x_r, c_s, c_r, px_s, px_r, pz_s, pz_r, hz_s, hz_r, hx_s, hx_r, y_s, y_r, f_s, f_r, a_s, a_r,
):
    x = lax.axis_index("dom")
    tp = lax.axis_index("tp")
    z = lax.axis_index("dp")
    core = lax.rem(tp, 2)
    y = lax.rem(tp // 2, 8)
    h = tp // 16

    def plane(i, j):
        return (lax.rem(x + i, 4), tp, lax.rem(z + j, 4))

    def chip(i, j):
        return (x, lax.rem(h + i, 2) * 16 + lax.rem(y + j, 8) * 2 + core, z)

    sibling = (x, tp + 1 - 2 * core, z)

    def send(src, dst, ss, rs, to):
        cp = pltpu.make_async_remote_copy(
            src_ref=src, dst_ref=dst, send_sem=ss, recv_sem=rs, device_id=to, device_id_type=MESH
        )
        cp.start()
        return cp

    loads = [
        pltpu.make_async_copy(src, dst, load_sem.at[n])
        for n, (src, dst) in enumerate(
            [(q_hbm.at[0], q), (k_hbm.at[0], k), (v_hbm.at[0], v), (wg_hbm, wg), (wu_hbm, wu), (wd_hbm, wd)]
        )
    ]
    for cp in loads:
        cp.start()

    barrier = pltpu.get_barrier_semaphore()
    partners = [chip(i, j) for i, j in CHIPS] + [sibling] + [plane(i, j) for i, j in PLANE]
    for to in partners:
        pl.semaphore_signal(barrier, inc=1, device_id=to, device_id_type=MESH)
    xp[0, 0, 0] = fold(rows_ref[...].astype(F32)).astype(BF16)
    pl.semaphore_wait(barrier, len(partners))

    xs = [
        send(xp.at[0, 0, 0], xp.at[0, i, j], x_s.at[i, j], x_r.at[i, j], chip(i, j)) for i, j in CHIPS
    ]

    p = x * 4 + z
    sub, lane = iota((16, 16), 0), iota((16, 16), 1)
    counts = jnp.broadcast_to(count_ref[...].astype(F32), (16, 16))
    count_col = jnp.sum(jnp.where(lane == sub, counts, 0.0), axis=1, keepdims=True)
    start_lane = jnp.sum(jnp.where(sub < lane, count_col, 0.0), axis=0, keepdims=True)
    end_lane = jnp.sum(jnp.where(sub <= lane, count_col, 0.0), axis=0, keepdims=True)
    start_col = jnp.sum(jnp.where(lane < sub, counts, 0.0), axis=1, keepdims=True)
    end_col = start_col + count_col
    block = (p * 4 + (iota((8, 16), 0) & 3)).astype(F32)
    mine = jnp.logical_and(start_lane <= block, block < end_lane)
    trim_of = jnp.sum(jnp.where(mine, trim_ref[...].astype(F32), 0.0), axis=1, keepdims=True)
    end_of = jnp.sum(jnp.where(mine, end_lane, 0.0), axis=1, keepdims=True)
    limit = jnp.where(block[:, :1] == end_of - 1.0, 128.0 - trim_of, 128.0)
    pos = iota((8, 512), 1)
    live = jnp.logical_and(pos // 128 == (iota((8, 512), 0) & 3), (pos & 127).astype(F32) < limit)
    bias8 = jnp.where(live, 0.0, NEG)
    bias = jnp.concatenate([bias8] * 8, axis=0)
    onehot = jnp.where(mine, 1.0, 0.0).astype(BF16)
    is_slot = (iota((64, 128), 0) & 7) < 4
    stat_lane = iota((64, 128), 1)

    for cp in loads[:3]:
        cp.wait()
    for n in range(KEY_HEADS):
        chosen = jnp.dot(onehot, q[:, n * 1024 : (n + 1) * 1024], preferred_element_type=F32)
        query = jnp.concatenate([chosen[:, j * 128 : (j + 1) * 128] for j in range(8)], axis=0).astype(BF16)
        scores = lax.dot_general(
            query, k[:, n * 128 : (n + 1) * 128], (((1,), (1,)), ((), ())), preferred_element_type=F32
        ) * (HEAD_SIZE ** -0.5) + bias
        top = jnp.max(scores, axis=1, keepdims=True).astype(BF16).astype(F32)
        weights = jnp.exp(scores - top).astype(BF16)
        total = jnp.sum(weights.astype(F32), axis=1, keepdims=True)
        total_hi = total.astype(BF16).astype(F32)
        numer = jnp.dot(weights, v[:, n * 128 : (n + 1) * 128], preferred_element_type=F32)
        stat = jnp.where(stat_lane < 32, top, jnp.where(stat_lane < 64, total_hi, total - total_hi))
        tile = jnp.where(is_slot, numer, stat).astype(BF16)
        asend[2 * n] = tile[:32]
        asend[2 * n + 1] = tile[32:]
    sends_a = [
        send(
            asend.at[lax.rem(x + i, 4) * 4 + lax.rem(z + j, 4)], ar.at[i * 4 + j],
            a_s.at[i * 4 + j], a_r.at[i * 4 + j], plane(i, j),
        )
        for i, j in PLANE
    ]
    ar[0] = asend[p]

    for cp in xs:
        cp.wait()
    to_sibling = send(xp.at[0], xp.at[1], c_s, c_r, sibling)

    def place(c):
        for i in range(2):
            for j in range(0, 8, 2):
                a, b = xp[c, i, j].astype(F32), xp[c, i, j + 1].astype(F32)
                at = i * 128 + c * 64 + j * 8
                xmat[at : at + 16, :256] = jnp.concatenate([a[:8], b[:8]], axis=0).astype(BF16)
                xmat[at : at + 16, 256:] = jnp.concatenate([a[8:], b[8:]], axis=0).astype(BF16)

    place(0)
    to_sibling.wait()
    place(1)

    loads[3].wait()
    loads[4].wait()
    for w, base in ((wg, 0), (wu, 896)):
        for lo, hi in ((0, 256), (256, 512), (512, 768), (768, 896)):
            part = jnp.dot(xmat[...], w[:, lo:hi], preferred_element_type=F32)
            psend[:, :, :, base + lo : base + hi] = part.astype(BF16).reshape(4, 4, 16, hi - lo)

    sends_px = [
        send(psend.at[lax.rem(x + i, 4)], xr.at[i], px_s.at[i], px_r.at[i], plane(i, 0)) for i in (2, 1, 3)
    ]

    for cp in sends_a:
        cp.wait()
    col = iota((16, 128), 1)
    from_block = ((((x + 4 - col // 32) & 3) * 4 + ((z + 4 - (col // 8 & 3)) & 3)) * 4 + (col & 3)).astype(F32)
    owns = jnp.logical_and(jnp.logical_and(start_col <= from_block, from_block < end_col), (col & 7) >= 4)
    gathered = ar[...].astype(F32)
    for j in range(4):
        part = gathered[:, j * 8 : (j + 1) * 8, :].reshape(128, 128)
        turned = part.T
        tops, totals = turned[0:1], turned[32:33] + turned[64:65]
        top = jnp.max(jnp.where(owns, tops, NEG), axis=1, keepdims=True)
        scale = jnp.exp(jnp.where(owns, tops - top, NEG))
        den = jnp.sum(scale * totals, axis=1, keepdims=True)
        num = jnp.dot(
            pltpu.roll(scale, 124, 1), part, precision=lax.Precision.HIGHEST, preferred_element_type=F32
        )
        attn_ref[0, :, j * 128 : (j + 1) * 128] = (num / den).astype(BF16)

    for cp in sends_px:
        cp.wait()

    def across_x(at):
        total = psend[x, at].astype(F32)
        for i in (1, 2, 3):
            total = total + xr[i, at].astype(F32)
        return total

    sends_pz = []
    for j in (2, 1, 3):
        at = lax.rem(z + j, 4)
        zsend[j] = across_x(at).astype(BF16)
        sends_pz.append(send(zsend.at[j], zr.at[j], pz_s.at[j], pz_r.at[j], plane(0, j)))
    summed = across_x(z)
    for cp in sends_pz:
        cp.wait()
    for j in (1, 2, 3):
        summed = summed + zr[j].astype(F32)
    gate, up = summed[:, :896], summed[:, 896:]
    hall[x, z] = (gate / (1.0 + jnp.exp(-gate)) * up).astype(BF16)

    for cp in [
        send(hall.at[x, z], hall.at[x, z], hz_s.at[j], hz_r.at[j], plane(0, j)) for j in (2, 1, 3)
    ]:
        cp.wait_send()
    for j in (1, 2, 3):
        at = lax.rem(z + 4 - j, 4)
        pltpu.make_async_copy(hall.at[x, at], hall.at[x, at], hz_r.at[j]).wait()
    for cp in [send(hall.at[x], hall.at[x], hx_s.at[i], hx_r.at[i], plane(i, 0)) for i in (2, 1, 3)]:
        cp.wait_send()
    for i in (1, 2, 3):
        at = lax.rem(x + 4 - i, 4)
        pltpu.make_async_copy(hall.at[at], hall.at[at], hx_r.at[i]).wait()

    loads[5].wait()
    down = jnp.dot(hall[...].reshape(256, 896), wd[...], preferred_element_type=F32)
    for i in range(2):
        ysend[i] = down[i * 128 + 64 : i * 128 + 128].astype(BF16)
    to_sibling = send(ysend, yr, y_s, y_r, sibling)
    to_sibling.wait()
    sends_f = []
    for i, j in CHIPS + [(0, 0)]:
        at = i * 128 + j * 8
        rows = down[at : at + 8] + yr[i, j * 8 // 16 * 16 : j * 8 // 16 * 16 + 16].astype(F32)[j % 2 * 8 : j % 2 * 8 + 8]
        piece = fold(rows)
        if i or j:
            fsend[i, j] = piece.astype(BF16)
            sends_f.append(send(fsend.at[i, j], fr.at[i, j], f_s.at[i, j], f_r.at[i, j], chip(2 - i, 8 - j)))
    for cp in sends_f:
        cp.wait()
    for i, j in CHIPS:
        piece = piece + fr[i, j].astype(F32)
    ffn_ref[...] = unfold(piece).astype(BF16)


def shards(query, key_block_pool, value_block_pool, row_blocks, trim, ffn_in, w_gate, w_up, w_down):
    any_ = pl.BlockSpec(memory_space=pl.ANY)
    vmem = pl.BlockSpec(memory_space=pltpu.VMEM)
    dma = pltpu.SemaphoreType.DMA
    return pl.pallas_call(
        kernel,
        out_shape=(jax.ShapeDtypeStruct((1, 16, 512), BF16), jax.ShapeDtypeStruct((8, 512), BF16)),
        in_specs=[any_, any_, any_, vmem, vmem, vmem, any_, any_, any_],
        out_specs=(vmem, vmem),
        scratch_shapes=[
            pltpu.VMEM((16, 8192), BF16),
            pltpu.VMEM((512, 1024), BF16),
            pltpu.VMEM((512, 1024), BF16),
            pltpu.VMEM((512, 896), BF16),
            pltpu.VMEM((512, 896), BF16),
            pltpu.VMEM((896, 512), BF16),
            pltpu.VMEM((2, 2, 8, 16, 256), BF16),
            pltpu.VMEM((256, 512), BF16),
            pltpu.VMEM((4, 4, 16, 1792), BF16),
            pltpu.VMEM((4, 4, 16, 1792), BF16),
            pltpu.VMEM((4, 16, 1792), BF16),
            pltpu.VMEM((4, 16, 1792), BF16),
            pltpu.VMEM((4, 4, 16, 896), BF16),
            pltpu.VMEM((2, 64, 512), BF16),
            pltpu.VMEM((2, 64, 512), BF16),
            pltpu.VMEM((2, 8, 16, 256), BF16),
            pltpu.VMEM((2, 8, 16, 256), BF16),
            pltpu.VMEM((16, 32, 128), BF16),
            pltpu.VMEM((16, 32, 128), BF16),
            dma((6,)),
            dma((2, 8)), dma((2, 8)),
            dma, dma,
            dma((4,)), dma((4,)),
            dma((4,)), dma((4,)),
            dma((4,)), dma((4,)),
            dma((4,)), dma((4,)),
            dma, dma,
            dma((2, 8)), dma((2, 8)),
            dma((16,)), dma((16,)),
        ],
        compiler_params=pltpu.CompilerParams(
            collective_id=0, has_side_effects=True, vmem_limit_bytes=48 << 20
        ),
        name="decode_step",
    )(query, key_block_pool, value_block_pool, row_blocks, trim, ffn_in, w_gate, w_up, w_down)


def solution(mesh):
    in_specs = (
        P("tp", None, None),
        P("tp", ("dom", "dp"), None),
        P("tp", ("dom", "dp"), None),
        P("tp", None),
        P("tp", None),
        P("tp", ("dom", "dp")),
        P(("dom", "dp"), "tp"),
        P(("dom", "dp"), "tp"),
        P("tp", ("dom", "dp")),
    )
    out_specs = (P("tp", None, ("dom", "dp")), P("tp", ("dom", "dp")))
    return jax.shard_map(shards, mesh=mesh, in_specs=in_specs, out_specs=out_specs, check_vma=False)
```

```python
import jax
import jax.numpy as jnp
from jax import lax
from jax.experimental import pallas as pl
from jax.experimental.pallas import tpu as pltpu
from jax.sharding import PartitionSpec as P

QUERY_HEADS = 64
KEY_HEADS = 8
HEAD_SIZE = 128
NEG = -1e30
MESH = pl.DeviceIdType.MESH
F32 = jnp.float32
BF16 = jnp.bfloat16

PLANE = [(i, j) for i in range(4) for j in range(4) if i or j]
CHIPS = [(i, j) for i in range(2) for j in range(8) if i or j]
PARTS = [(0, 0, 512), (1, 0, 512), (1, 512, 384), (0, 512, 384)]


def iota(shape, axis):
    return lax.broadcasted_iota(jnp.int32, shape, axis)


def fold(rows):
    return jnp.concatenate([rows[:, :256], rows[:, 256:]], axis=0)


def unfold(piece):
    return jnp.concatenate([piece[:8], piece[8:]], axis=1)


def kernel(
    q_hbm, k_hbm, v_hbm, count_ref, trim_ref, rows_ref, wg_hbm, wu_hbm, wd_hbm,
    attn_ref, ffn_ref,
    q, k, v, wg, wu, wd,
    xp, xmat, psend_0, psend_1, psend_2, psend_3, xr_0, xr_1, xr_2, xr_3, zsend, zr, hall, down, ysend, yr, fsend, fr, asend, ar,
    load_sem, x_s, x_r, c_s, c_r, px_s, px_r, pz_s, pz_r, hz_s, hz_r, hx_s, hx_r, y_s, y_r, f_s, f_r, a_s, a_r,
):
    psend, xr = (psend_0, psend_1, psend_2, psend_3), (xr_0, xr_1, xr_2, xr_3)
    x = lax.axis_index("dom")
    tp = lax.axis_index("tp")
    z = lax.axis_index("dp")
    core = lax.rem(tp, 2)
    y = lax.rem(tp // 2, 8)
    h = tp // 16

    def plane(i, j):
        return (lax.rem(x + i, 4), tp, lax.rem(z + j, 4))

    def chip(i, j):
        return (x, lax.rem(h + i, 2) * 16 + lax.rem(y + j, 8) * 2 + core, z)

    sibling = (x, tp + 1 - 2 * core, z)

    def send(src, dst, ss, rs, to):
        cp = pltpu.make_async_remote_copy(
            src_ref=src, dst_ref=dst, send_sem=ss, recv_sem=rs, device_id=to, device_id_type=MESH
        )
        cp.start()
        return cp

    def arrived(ref, sem):
        pltpu.make_async_copy(ref, ref, sem).wait()

    loads = [
        pltpu.make_async_copy(src, dst, load_sem.at[n])
        for n, (src, dst) in enumerate(
            [(q_hbm.at[0], q), (k_hbm.at[0], k), (v_hbm.at[0], v), (wg_hbm, wg), (wu_hbm, wu), (wd_hbm, wd)]
        )
    ]
    for cp in loads:
        cp.start()

    barrier = pltpu.get_barrier_semaphore()
    partners = [chip(i, j) for i, j in CHIPS] + [sibling] + [plane(i, j) for i, j in PLANE]
    for to in partners:
        pl.semaphore_signal(barrier, inc=1, device_id=to, device_id_type=MESH)
    xp[0, 0, 0] = fold(rows_ref[...].astype(F32)).astype(BF16)
    pl.semaphore_wait(barrier, len(partners))

    xs = {
        (i, j): send(xp.at[0, 0, 0], xp.at[i, 0, j], x_s.at[i, j], x_r.at[i, j], chip(i, j))
        for i, j in CHIPS
    }

    p = x * 4 + z
    sub, lane = iota((16, 16), 0), iota((16, 16), 1)
    counts = jnp.broadcast_to(count_ref[...].astype(F32), (16, 16))
    count_col = jnp.sum(jnp.where(lane == sub, counts, 0.0), axis=1, keepdims=True)
    start_lane = jnp.sum(jnp.where(sub < lane, count_col, 0.0), axis=0, keepdims=True)
    end_lane = jnp.sum(jnp.where(sub <= lane, count_col, 0.0), axis=0, keepdims=True)
    start_col = jnp.sum(jnp.where(lane < sub, counts, 0.0), axis=1, keepdims=True)
    end_col = start_col + count_col
    block = (p * 4 + (iota((8, 16), 0) & 3)).astype(F32)
    mine = jnp.logical_and(start_lane <= block, block < end_lane)
    trim_of = jnp.sum(jnp.where(mine, trim_ref[...].astype(F32), 0.0), axis=1, keepdims=True)
    end_of = jnp.sum(jnp.where(mine, end_lane, 0.0), axis=1, keepdims=True)
    limit = jnp.where(block[:, :1] == end_of - 1.0, 128.0 - trim_of, 128.0)
    pos = iota((8, 512), 1)
    live = jnp.logical_and(pos // 128 == (iota((8, 512), 0) & 3), (pos & 127).astype(F32) < limit)
    bias8 = jnp.where(live, 0.0, NEG)
    bias = jnp.concatenate([bias8] * 8, axis=0)
    onehot = jnp.where(mine, 1.0, 0.0).astype(BF16)
    is_slot = (iota((64, 128), 0) & 7) < 4
    stat_lane = iota((64, 128), 1)

    for cp in loads[:3]:
        cp.wait()
    for n in range(KEY_HEADS):
        chosen = jnp.dot(onehot, q[:, n * 1024 : (n + 1) * 1024], preferred_element_type=F32)
        query = jnp.concatenate([chosen[:, j * 128 : (j + 1) * 128] for j in range(8)], axis=0).astype(BF16)
        scores = lax.dot_general(
            query, k[:, n * 128 : (n + 1) * 128], (((1,), (1,)), ((), ())), preferred_element_type=F32
        ) * (HEAD_SIZE ** -0.5) + bias
        top = jnp.max(scores, axis=1, keepdims=True).astype(BF16).astype(F32)
        weights = jnp.exp(scores - top).astype(BF16)
        total = jnp.sum(weights.astype(F32), axis=1, keepdims=True)
        total_hi = total.astype(BF16).astype(F32)
        numer = jnp.dot(weights, v[:, n * 128 : (n + 1) * 128], preferred_element_type=F32)
        stat = jnp.where(stat_lane < 32, top, jnp.where(stat_lane < 64, total_hi, total - total_hi))
        tile = jnp.where(is_slot, numer, stat).astype(BF16)
        asend[2 * n] = tile[:32]
        asend[2 * n + 1] = tile[32:]
    def gather(half):
        for j in range(8):
            if half or j:
                xs[half, j].wait()
        to_sibling = send(xp.at[half, 0], xp.at[half, 1], c_s.at[half], c_r.at[half], sibling)
        for c in range(2):
            if c:
                to_sibling.wait()
            for j in range(0, 8, 2):
                a, b = xp[half, c, j].astype(F32), xp[half, c, j + 1].astype(F32)
                at = half * 128 + c * 64 + j * 8
                xmat[at : at + 16, :256] = jnp.concatenate([a[:8], b[:8]], axis=0).astype(BF16)
                xmat[at : at + 16, 256:] = jnp.concatenate([a[8:], b[8:]], axis=0).astype(BF16)

    def gate_up(n):
        half, first, units = PARTS[n]
        rows = xmat[half * 128 : half * 128 + 128, :]
        for lo in range(0, units, 256):
            wide = min(256, units - lo)
            g = jnp.dot(rows, wg[:, first + lo : first + lo + wide], preferred_element_type=F32)
            u = jnp.dot(rows, wu[:, first + lo : first + lo + wide], preferred_element_type=F32)
            both = jnp.concatenate([g.reshape(16, 8, wide), u.reshape(16, 8, wide)], axis=1)
            psend[n][:, :, :, lo : lo + wide] = both.astype(BF16).reshape(4, 4, 16, wide)
        return [
            send(psend[n].at[lax.rem(x + i, 4)], xr[n].at[i], px_s.at[n, i], px_r.at[n, i], plane(i, 0))
            for i in (2, 1, 3)
        ]

    kept = {}

    def over_x(n, copies):
        units = PARTS[n][2]
        for cp in copies:
            cp.wait()

        def total(at):
            value = psend[n][x, at].astype(F32)
            for i in (1, 2, 3):
                value = value + xr[n][i, at].astype(F32)
            return value

        out = []
        for j in (2, 1, 3):
            zsend[n, j, :, :units] = total(lax.rem(z + j, 4)).astype(BF16)
            out.append(
                send(
                    zsend.at[n, j, :, pl.ds(0, units)], zr.at[n, j, :, pl.ds(0, units)],
                    pz_s.at[n, j], pz_r.at[n, j], plane(0, j),
                )
            )
        kept[n] = total(z)
        return out

    def over_z(n, copies):
        units = PARTS[n][2]
        for cp in copies:
            cp.wait()
        value = kept[n]
        for j in (1, 2, 3):
            value = value + zr[n, j, :, :units].astype(F32)
        gate, up = value[:8], value[8:]
        hidden = gate / (1.0 + jnp.exp(-gate)) * up
        if units < 512:
            hidden = jnp.concatenate([hidden, jnp.zeros((8, 512 - units), F32)], axis=1)
        hall[n, x, z] = fold(hidden).astype(BF16)
        return [
            send(hall.at[n, x, z], hall.at[n, x, z], hz_s.at[n, j], hz_r.at[n, j], plane(0, j))
            for j in (2, 1, 3)
        ]

    def gather_z(n, copies):
        for cp in copies:
            cp.wait_send()
        for j in (1, 2, 3):
            arrived(hall.at[n, x, lax.rem(z + 4 - j, 4)], hz_r.at[n, j])
        return [
            send(hall.at[n, x], hall.at[n, x], hx_s.at[n, i], hx_r.at[n, i], plane(i, 0)) for i in (2, 1, 3)
        ]

    def gather_x(n, copies):
        half, first, units = PARTS[n]
        for cp in copies:
            cp.wait_send()
        for i in (1, 2, 3):
            arrived(hall.at[n, lax.rem(x + 4 - i, 4)], hx_r.at[n, i])
        rows = hall[n].astype(F32).reshape(16, 16, 256)
        left = rows[:, :8].reshape(128, 256).astype(BF16)
        right = rows[:, 8:].reshape(128, 256).astype(BF16)[:, : units - 256]
        return jnp.dot(left, wd[first : first + 256, :], preferred_element_type=F32) + jnp.dot(
            right, wd[first + 256 : first + units, :], preferred_element_type=F32
        )

    def other_core(half, rows):
        down[half] = rows[:64]
        ysend[half] = rows[64:].astype(BF16)
        return send(ysend.at[half], yr.at[half], y_s.at[half], y_r.at[half], sibling)

    def owners(half, copy):
        copy.wait()
        rows = down[half] + yr[half].astype(F32)
        out = []
        for j in range(8):
            piece = fold(rows[j * 8 : j * 8 + 8])
            if half == 0 and j == 0:
                kept["own"] = piece
                continue
            fsend[half, j] = piece.astype(BF16)
            out.append(
                send(fsend.at[half, j], fr.at[half, j], f_s.at[half, j], f_r.at[half, j], chip(2 - half, 8 - j))
            )
        return out

    gather(0)
    loads[3].wait()
    loads[4].wait()
    px = {0: gate_up(0)}
    gather(1)
    px[1] = gate_up(1)
    px[2] = gate_up(2)
    px[3] = gate_up(3)
    pz = {0: over_x(0, px[0])}
    pz[1] = over_x(1, px[1])
    hz = {0: over_z(0, pz[0])}
    pz[2] = over_x(2, px[2])
    hz[1] = over_z(1, pz[1])
    hx = {0: gather_z(0, hz[0])}
    pz[3] = over_x(3, px[3])
    hz[2] = over_z(2, pz[2])
    hx[1] = gather_z(1, hz[1])
    hz[3] = over_z(3, pz[3])
    hx[2] = gather_z(2, hz[2])
    loads[5].wait()
    rows_b = gather_x(1, hx[1])
    rows_a = gather_x(0, hx[0])
    hx[3] = gather_z(3, hz[3])
    sends_a = [
        send(
            asend.at[lax.rem(x + i, 4) * 4 + lax.rem(z + j, 4)], ar.at[i * 4 + j],
            a_s.at[i * 4 + j], a_r.at[i * 4 + j], plane(i, j),
        )
        for i, j in PLANE
    ]
    ar[0] = asend[p]

    to_core = other_core(1, rows_b + gather_x(2, hx[2]))
    sends_b = owners(1, to_core)
    to_core = other_core(0, rows_a + gather_x(3, hx[3]))
    sends_f = sends_b + owners(0, to_core)
    for cp in sends_a:
        cp.wait()
    col = iota((16, 128), 1)
    from_block = ((((x + 4 - col // 32) & 3) * 4 + ((z + 4 - (col // 8 & 3)) & 3)) * 4 + (col & 3)).astype(F32)
    owns = jnp.logical_and(jnp.logical_and(start_col <= from_block, from_block < end_col), (col & 7) >= 4)
    gathered = ar[...].astype(F32)
    for j in range(4):
        part = gathered[:, j * 8 : (j + 1) * 8, :].reshape(128, 128)
        turned = part.T
        tops, totals = turned[0:1], turned[32:33] + turned[64:65]
        top = jnp.max(jnp.where(owns, tops, NEG), axis=1, keepdims=True)
        scale = jnp.exp(jnp.where(owns, tops - top, NEG))
        den = jnp.sum(scale * totals, axis=1, keepdims=True)
        num = jnp.dot(
            pltpu.roll(scale, 124, 1), part, precision=lax.Precision.HIGHEST, preferred_element_type=F32
        )
        attn_ref[0, :, j * 128 : (j + 1) * 128] = (num / den).astype(BF16)

    for cp in sends_f:
        cp.wait()
    piece = kept["own"]
    for i, j in CHIPS:
        piece = piece + fr[i, j].astype(F32)
    ffn_ref[...] = unfold(piece).astype(BF16)


def shards(query, key_block_pool, value_block_pool, row_blocks, trim, ffn_in, w_gate, w_up, w_down):
    any_ = pl.BlockSpec(memory_space=pl.ANY)
    vmem = pl.BlockSpec(memory_space=pltpu.VMEM)
    dma = pltpu.SemaphoreType.DMA
    return pl.pallas_call(
        kernel,
        out_shape=(jax.ShapeDtypeStruct((1, 16, 512), BF16), jax.ShapeDtypeStruct((8, 512), BF16)),
        in_specs=[any_, any_, any_, vmem, vmem, vmem, any_, any_, any_],
        out_specs=(vmem, vmem),
        scratch_shapes=[
            pltpu.VMEM((16, 8192), BF16),
            pltpu.VMEM((512, 1024), BF16),
            pltpu.VMEM((512, 1024), BF16),
            pltpu.VMEM((512, 896), BF16),
            pltpu.VMEM((512, 896), BF16),
            pltpu.VMEM((896, 512), BF16),
            pltpu.VMEM((2, 2, 8, 16, 256), BF16),
            pltpu.VMEM((256, 512), BF16),
            *[pltpu.VMEM((4, 4, 16, part[2]), BF16) for part in PARTS],
            *[pltpu.VMEM((4, 4, 16, part[2]), BF16) for part in PARTS],
            pltpu.VMEM((4, 4, 16, 512), BF16),
            pltpu.VMEM((4, 4, 16, 512), BF16),
            pltpu.VMEM((4, 4, 4, 16, 256), BF16),
            pltpu.VMEM((2, 64, 512), F32),
            pltpu.VMEM((2, 64, 512), BF16),
            pltpu.VMEM((2, 64, 512), BF16),
            pltpu.VMEM((2, 8, 16, 256), BF16),
            pltpu.VMEM((2, 8, 16, 256), BF16),
            pltpu.VMEM((16, 32, 128), BF16),
            pltpu.VMEM((16, 32, 128), BF16),
            dma((6,)),
            dma((2, 8)), dma((2, 8)),
            dma((2,)), dma((2,)),
            dma((4, 4)), dma((4, 4)),
            dma((4, 4)), dma((4, 4)),
            dma((4, 4)), dma((4, 4)),
            dma((4, 4)), dma((4, 4)),
            dma((2,)), dma((2,)),
            dma((2, 8)), dma((2, 8)),
            dma((16,)), dma((16,)),
        ],
        compiler_params=pltpu.CompilerParams(
            collective_id=0, has_side_effects=True, vmem_limit_bytes=60 << 20
        ),
        name="decode_step",
    )(query, key_block_pool, value_block_pool, row_blocks, trim, ffn_in, w_gate, w_up, w_down)


def solution(mesh):
    in_specs = (
        P("tp", None, None),
        P("tp", ("dom", "dp"), None),
        P("tp", ("dom", "dp"), None),
        P("tp", None),
        P("tp", None),
        P("tp", ("dom", "dp")),
        P(("dom", "dp"), "tp"),
        P(("dom", "dp"), "tp"),
        P("tp", ("dom", "dp")),
    )
    out_specs = (P("tp", None, ("dom", "dp")), P("tp", ("dom", "dp")))
    return jax.shard_map(shards, mesh=mesh, in_specs=in_specs, out_specs=out_specs, check_vma=False)
```

```python
import jax
import jax.numpy as jnp
from jax import lax
from jax.experimental import pallas as pl
from jax.experimental.pallas import tpu as pltpu
from jax.sharding import PartitionSpec as P

QUERY_HEADS = 64
KEY_HEADS = 8
HEAD_SIZE = 128
NEG = -1e30
MESH = pl.DeviceIdType.MESH
F32 = jnp.float32
BF16 = jnp.bfloat16

PLANE = [(i, j) for i in range(4) for j in range(4) if i or j]
CHIPS = [(i, j) for i in range(2) for j in range(8) if i or j]

FAR_FIRST = sorted(PLANE, key=lambda t: -(min(t[0], 4 - t[0]) + min(t[1], 4 - t[1])))
DIRECT = (3,)


def iota(shape, axis):
    return lax.broadcasted_iota(jnp.int32, shape, axis)


def fold(rows):
    return jnp.concatenate([rows[:, :256], rows[:, 256:]], axis=0)


def unfold(piece):
    return jnp.concatenate([piece[:8], piece[8:]], axis=1)


def kernel(
    q_hbm, k_hbm, v_hbm, count_ref, trim_ref, rows_ref, wg_hbm, wu_hbm, wd_hbm,
    attn_ref, ffn_ref,
    q, k, v, wg, wu, wd,
    xp, xmat, psend, xr, ztotal, zsend, zr, hall, down, ysend, yr, fsend, fr, asend, ar,
    load_sem, x_s, x_r, c_s, c_r, px_s, px_r, pz_s, pz_r, hz_s, hz_r, hx_s, hx_r, hd_s, hd_r, y_s, y_r, f_s, f_r, a_s, a_r,
):
    x = lax.axis_index("dom")
    tp = lax.axis_index("tp")
    z = lax.axis_index("dp")
    core = lax.rem(tp, 2)
    y = lax.rem(tp // 2, 8)
    h = tp // 16

    def plane(i, j):
        return (lax.rem(x + i, 4), tp, lax.rem(z + j, 4))

    def chip(i, j):
        return (x, lax.rem(h + i, 2) * 16 + lax.rem(y + j, 8) * 2 + core, z)

    sibling = (x, tp + 1 - 2 * core, z)

    def send(src, dst, ss, rs, to):
        cp = pltpu.make_async_remote_copy(
            src_ref=src, dst_ref=dst, send_sem=ss, recv_sem=rs, device_id=to, device_id_type=MESH
        )
        cp.start()
        return cp

    def arrived(ref, sem):
        pltpu.make_async_copy(ref, ref, sem).wait()

    barrier = pltpu.get_barrier_semaphore()
    partners = (
        [chip(0, j) for j in range(1, 8)] + [chip(1, 0), sibling]
        + [plane(i, 0) for i in (1, 2, 3)] + [plane(0, j) for j in (1, 2, 3)]
    )
    for to in partners:
        pl.semaphore_signal(barrier, inc=1, device_id=to, device_id_type=MESH)
    loads = [
        pltpu.make_async_copy(src, dst, load_sem.at[n])
        for n, (src, dst) in enumerate(
            [(q_hbm.at[0], q), (k_hbm.at[0], k), (v_hbm.at[0], v), (wg_hbm, wg), (wu_hbm, wu), (wd_hbm, wd)]
        )
    ]
    for cp in loads:
        cp.start()
    xp[0, 0, 0] = fold(rows_ref[...].astype(F32)).astype(BF16)

    p = x * 4 + z
    sub, lane = iota((16, 16), 0), iota((16, 16), 1)
    counts = jnp.broadcast_to(count_ref[...].astype(F32), (16, 16))
    count_col = jnp.sum(jnp.where(lane == sub, counts, 0.0), axis=1, keepdims=True)
    start_lane = jnp.sum(jnp.where(sub < lane, count_col, 0.0), axis=0, keepdims=True)
    end_lane = jnp.sum(jnp.where(sub <= lane, count_col, 0.0), axis=0, keepdims=True)
    start_col = jnp.sum(jnp.where(lane < sub, counts, 0.0), axis=1, keepdims=True)
    end_col = start_col + count_col
    block = (p * 4 + (iota((8, 16), 0) & 3)).astype(F32)
    mine = jnp.logical_and(start_lane <= block, block < end_lane)
    trim_of = jnp.sum(jnp.where(mine, trim_ref[...].astype(F32), 0.0), axis=1, keepdims=True)
    end_of = jnp.sum(jnp.where(mine, end_lane, 0.0), axis=1, keepdims=True)
    limit = jnp.where(block[:, :1] == end_of - 1.0, 128.0 - trim_of, 128.0)
    pos = iota((8, 512), 1)
    live = jnp.logical_and(pos // 128 == (iota((8, 512), 0) & 3), (pos & 127).astype(F32) < limit)
    bias8 = jnp.where(live, 0.0, NEG)
    bias = jnp.concatenate([bias8] * 8, axis=0)
    onehot = jnp.where(mine, 1.0, 0.0).astype(BF16)
    is_slot = (iota((64, 128), 0) & 7) < 4
    stat_lane = iota((64, 128), 1)

    for cp in loads[:3]:
        cp.wait()
    def attend(first, last):
        for n in range(first, last):
            chosen = jnp.dot(onehot, q[:, n * 1024 : (n + 1) * 1024], preferred_element_type=F32)
            query = jnp.concatenate([chosen[:, j * 128 : (j + 1) * 128] for j in range(8)], axis=0).astype(BF16)
            scores = lax.dot_general(
                query, k[:, n * 128 : (n + 1) * 128], (((1,), (1,)), ((), ())), preferred_element_type=F32
            ) * (HEAD_SIZE ** -0.5) + bias
            top = jnp.max(scores, axis=1, keepdims=True).astype(BF16).astype(F32)
            weights = jnp.exp(scores - top).astype(BF16)
            total = jnp.sum(weights.astype(F32), axis=1, keepdims=True)
            total_hi = total.astype(BF16).astype(F32)
            numer = jnp.dot(weights, v[:, n * 128 : (n + 1) * 128], preferred_element_type=F32)
            stat = jnp.where(stat_lane < 32, top, jnp.where(stat_lane < 64, total_hi, total - total_hi))
            tile = jnp.where(is_slot, numer, stat).astype(BF16)
            asend[2 * n] = tile[:32]
            asend[2 * n + 1] = tile[32:]

    attend(0, 0)
    pl.semaphore_wait(barrier, len(partners))

    xs = {}
    xs[1, 0] = send(xp.at[0, 0, 0], xp.at[1, 0, 0], x_s.at[1, 0], x_r.at[1, 0], chip(1, 0))
    for j in (4, 3, 5, 2, 6, 1, 7):
        xs[0, j] = send(xp.at[0, 0, 0], xp.at[0, 0, j], x_s.at[0, j], x_r.at[0, j], chip(0, j))

    attend(0, KEY_HEADS)

    def put(half, c):
        for j in range(0, 8, 2):
            a, b = xp[half, c, j].astype(F32), xp[half, c, j + 1].astype(F32)
            xmat[2 * half + c, j * 8 : j * 8 + 16, :256] = jnp.concatenate([a[:8], b[:8]], axis=0).astype(BF16)
            xmat[2 * half + c, j * 8 : j * 8 + 16, 256:] = jnp.concatenate([a[8:], b[8:]], axis=0).astype(BF16)

    def to_other_core(half):
        return send(xp.at[half, 0], xp.at[half, 1], c_s.at[half], c_r.at[half], sibling)

    def gate_up(n):
        rows = xmat[n]
        for lo, hi in ((0, 256), (256, 512), (512, 768), (768, 896)):
            g = jnp.dot(rows, wg[:, lo:hi], preferred_element_type=F32)
            u = jnp.dot(rows, wu[:, lo:hi], preferred_element_type=F32)
            both = jnp.concatenate([g.reshape(8, 8, hi - lo), u.reshape(8, 8, hi - lo)], axis=1)
            psend[n, :, :, :, lo:hi] = both.astype(BF16).reshape(4, 2, 16, hi - lo)
        return [
            send(psend.at[n, lax.rem(x + i, 4)], xr.at[n, i], px_s.at[n, i], px_r.at[n, i], plane(i, 0))
            for i in (2, 1, 3)
        ]

    def over_x(n, copies):
        for cp in copies:
            cp.wait()
        for r in range(2):
            value = psend[n, x, r].astype(F32)
            for i in (1, 2, 3):
                value = value + xr[n, i, r].astype(F32)
            ztotal[n, 2 * r] = value[:, :512]
            ztotal[n, 2 * r + 1, :, :384] = value[:, 512:]
            ztotal[n, 2 * r + 1, :, 384:] = jnp.zeros((16, 128), F32)
            zsend[n, 2 * r] = value[:, :512].astype(BF16)
            zsend[n, 2 * r + 1, :, :384] = value[:, 512:].astype(BF16)
            zsend[n, 2 * r + 1, :, 384:] = jnp.zeros((16, 128), BF16)
        return [
            send(zsend.at[n, lax.rem(z + j, 4)], zr.at[n, j], pz_s.at[n, j], pz_r.at[n, j], plane(0, j))
            for j in (2, 1, 3)
        ]

    def over_z(n, copies):
        for cp in copies:
            cp.wait()
        value = ztotal[n, z]
        for j in (1, 2, 3):
            value = value + zr[n, j].astype(F32)
        gate, up = value[:8], value[8:]
        hall[n, x, z] = fold(gate / (1.0 + jnp.exp(-gate)) * up).astype(BF16)
        if n in DIRECT:
            return [
                send(hall.at[n, x, z], hall.at[n, x, z], hd_s.at[n, i * 4 + j], hd_r.at[n, i * 4 + j], plane(i, j))
                for i, j in FAR_FIRST
            ]
        return [
            send(hall.at[n, x, z], hall.at[n, x, z], hz_s.at[n, j], hz_r.at[n, j], plane(0, j))
            for j in (2, 1, 3)
        ]

    def gather_z(n, copies):
        if n in DIRECT:
            return copies
        for cp in copies:
            cp.wait_send()
        for j in (1, 2, 3):
            arrived(hall.at[n, x, lax.rem(z + 4 - j, 4)], hz_r.at[n, j])
        return [
            send(hall.at[n, x], hall.at[n, x], hx_s.at[n, i], hx_r.at[n, i], plane(i, 0)) for i in (2, 1, 3)
        ]

    def gather_x(n, copies):
        for cp in copies:
            cp.wait_send()
        if n in DIRECT:
            for i, j in FAR_FIRST:
                arrived(hall.at[n, lax.rem(x + 4 - i, 4), lax.rem(z + 4 - j, 4)], hd_r.at[n, i * 4 + j])
        else:
            for i in (1, 2, 3):
                arrived(hall.at[n, lax.rem(x + 4 - i, 4)], hx_r.at[n, i])
        rows = hall[n].astype(F32).reshape(8, 2, 2, 8, 256)
        out = 0.0
        for i, lo, hi in ((0, 0, 256), (1, 256, 512), (2, 512, 768), (3, 768, 896)):
            part = rows[:, i // 2, i % 2].reshape(64, 256).astype(BF16)[:, : hi - lo]
            out = out + jnp.dot(part, wd[lo:hi, :], preferred_element_type=F32)
        return out

    def other_core(half, rows):
        ysend[half] = rows.astype(BF16)
        return send(ysend.at[half], yr.at[half], y_s.at[half], y_r.at[half], sibling)

    kept = {}

    def owners(half, copy):
        copy.wait()
        rows = down[half] + yr[half].astype(F32)
        out = []
        for j in range(8):
            piece = fold(rows[j * 8 : j * 8 + 8])
            if half == 0 and j == 0:
                kept["own"] = piece
                continue
            fsend[half, j] = piece.astype(BF16)
            out.append(
                send(fsend.at[half, j], fr.at[half, j], f_s.at[half, j], f_r.at[half, j], chip(2 - half, 8 - j))
            )
        return out

    xs[1, 0].wait()
    for j in (4, 3, 5, 2, 6, 1, 7):
        xs[1, j] = send(xp.at[1, 0, 0], xp.at[1, 0, j], x_s.at[1, j], x_r.at[1, j], chip(0, j))
    for j in range(1, 8):
        xs[0, j].wait()
    cores_a = to_other_core(0)
    put(0, 0)
    loads[3].wait()
    loads[4].wait()
    px = {0: gate_up(0)}
    cores_a.wait()
    put(0, 1)
    px[1] = gate_up(1)
    for j in range(1, 8):
        xs[1, j].wait()
    cores_b = to_other_core(1)
    put(1, 0)
    px[2] = gate_up(2)
    cores_b.wait()
    put(1, 1)
    px[3] = gate_up(3)
    pz = {0: over_x(0, px[0])}
    pz[1] = over_x(1, px[1])
    hz = {0: over_z(0, pz[0])}
    pz[2] = over_x(2, px[2])
    hz[1] = over_z(1, pz[1])
    hx = {0: gather_z(0, hz[0])}
    pz[3] = over_x(3, px[3])
    hz[2] = over_z(2, pz[2])
    hx[1] = gather_z(1, hz[1])
    hz[3] = over_z(3, pz[3])
    hx[2] = gather_z(2, hz[2])
    loads[5].wait()
    down[0] = gather_x(0, hx[0])
    core_a = other_core(0, gather_x(1, hx[1]))
    hx[3] = gather_z(3, hz[3])
    sends_f = owners(0, core_a)
    down[1] = gather_x(2, hx[2])
    core_b = other_core(1, gather_x(3, hx[3]))
    sends_a = [
        send(
            asend.at[lax.rem(x + i, 4) * 4 + lax.rem(z + j, 4)], ar.at[i * 4 + j],
            a_s.at[i * 4 + j], a_r.at[i * 4 + j], plane(i, j),
        )
        for i, j in PLANE
    ]
    ar[0] = asend[p]

    sends_f = sends_f + owners(1, core_b)
    for cp in sends_a:
        cp.wait()
    col = iota((16, 128), 1)
    from_block = ((((x + 4 - col // 32) & 3) * 4 + ((z + 4 - (col // 8 & 3)) & 3)) * 4 + (col & 3)).astype(F32)
    owns = jnp.logical_and(jnp.logical_and(start_col <= from_block, from_block < end_col), (col & 7) >= 4)
    gathered = ar[...].astype(F32)
    for j in range(4):
        part = gathered[:, j * 8 : (j + 1) * 8, :].reshape(128, 128)
        turned = part.T
        tops, totals = turned[0:1], turned[32:33] + turned[64:65]
        top = jnp.max(jnp.where(owns, tops, NEG), axis=1, keepdims=True)
        scale = jnp.exp(jnp.where(owns, tops - top, NEG))
        den = jnp.sum(scale * totals, axis=1, keepdims=True)
        num = jnp.dot(
            pltpu.roll(scale, 124, 1), part, precision=lax.Precision.HIGHEST, preferred_element_type=F32
        )
        attn_ref[0, :, j * 128 : (j + 1) * 128] = (num / den).astype(BF16)

    for cp in sends_f:
        cp.wait()
    piece = kept["own"]
    for i, j in CHIPS:
        piece = piece + fr[i, j].astype(F32)
    ffn_ref[...] = unfold(piece).astype(BF16)


def shards(query, key_block_pool, value_block_pool, row_blocks, trim, ffn_in, w_gate, w_up, w_down):
    any_ = pl.BlockSpec(memory_space=pl.ANY)
    vmem = pl.BlockSpec(memory_space=pltpu.VMEM)
    dma = pltpu.SemaphoreType.DMA
    return pl.pallas_call(
        kernel,
        out_shape=(pltpu.VMEM((1, 16, 512), BF16), pltpu.VMEM((8, 512), BF16)),
        in_specs=[any_, any_, any_, vmem, vmem, vmem, any_, any_, any_],
        out_specs=(vmem, vmem),
        scratch_shapes=[
            pltpu.VMEM((16, 8192), BF16),
            pltpu.VMEM((512, 1024), BF16),
            pltpu.VMEM((512, 1024), BF16),
            pltpu.VMEM((512, 896), BF16),
            pltpu.VMEM((512, 896), BF16),
            pltpu.VMEM((896, 512), BF16),
            pltpu.VMEM((2, 2, 8, 16, 256), BF16),
            pltpu.VMEM((4, 64, 512), BF16),
            pltpu.VMEM((4, 4, 2, 16, 896), BF16),
            pltpu.VMEM((4, 4, 2, 16, 896), BF16),
            pltpu.VMEM((4, 4, 16, 512), F32),
            pltpu.VMEM((4, 4, 16, 512), BF16),
            pltpu.VMEM((4, 4, 16, 512), BF16),
            pltpu.VMEM((4, 4, 4, 16, 256), BF16),
            pltpu.VMEM((2, 64, 512), F32),
            pltpu.VMEM((2, 64, 512), BF16),
            pltpu.VMEM((2, 64, 512), BF16),
            pltpu.VMEM((2, 8, 16, 256), BF16),
            pltpu.VMEM((2, 8, 16, 256), BF16),
            pltpu.VMEM((16, 32, 128), BF16),
            pltpu.VMEM((16, 32, 128), BF16),
            dma((6,)),
            dma((2, 8)), dma((2, 8)),
            dma((2,)), dma((2,)),
            dma((4, 4)), dma((4, 4)),
            dma((4, 4)), dma((4, 4)),
            dma((4, 4)), dma((4, 4)),
            dma((4, 4)), dma((4, 4)),
            dma((4, 16)), dma((4, 16)),
            dma((2,)), dma((2,)),
            dma((2, 8)), dma((2, 8)),
            dma((16,)), dma((16,)),
        ],
        compiler_params=pltpu.CompilerParams(
            collective_id=0, has_side_effects=True, vmem_limit_bytes=60 << 20
        ),
        name="decode_step",
    )(query, key_block_pool, value_block_pool, row_blocks, trim, ffn_in, w_gate, w_up, w_down)


def solution(mesh):
    in_specs = (
        P("tp", None, None),
        P("tp", ("dom", "dp"), None),
        P("tp", ("dom", "dp"), None),
        P("tp", None),
        P("tp", None),
        P("tp", ("dom", "dp")),
        P(("dom", "dp"), "tp"),
        P(("dom", "dp"), "tp"),
        P("tp", ("dom", "dp")),
    )
    out_specs = (P("tp", None, ("dom", "dp")), P("tp", ("dom", "dp")))
    return jax.shard_map(shards, mesh=mesh, in_specs=in_specs, out_specs=out_specs, check_vma=False)
```

```python
import jax
import jax.numpy as jnp
from jax import lax
from jax.experimental import pallas as pl
from jax.experimental.pallas import tpu as pltpu
from jax.sharding import PartitionSpec as P

QUERY_HEADS = 64
KEY_HEADS = 8
HEAD_SIZE = 128
NEG = -1e30
MESH = pl.DeviceIdType.MESH
F32 = jnp.float32
BF16 = jnp.bfloat16

PLANE = [(i, j) for i in range(4) for j in range(4) if i or j]
CHIPS = [(i, j) for i in range(2) for j in range(8) if i or j]

FAR_FIRST = sorted(PLANE, key=lambda t: -(min(t[0], 4 - t[0]) + min(t[1], 4 - t[1])))
DIRECT = (2, 3,)
FAR, NEAR = (4, 3, 5, 2), (6, 1, 7, 0)
PARTS = (
    (0, [(0, j) for j in range(8)]),
    (0, [(1, j) for j in range(8)]),
    (1, [(c, j) for c in (0, 1) for j in FAR]),
    (1, [(c, j) for c in (0, 1) for j in NEAR]),
)


def iota(shape, axis):
    return lax.broadcasted_iota(jnp.int32, shape, axis)


def fold(rows):
    return jnp.concatenate([rows[:, :256], rows[:, 256:]], axis=0)


def unfold(piece):
    return jnp.concatenate([piece[:8], piece[8:]], axis=1)


def kernel(
    q_hbm, k_hbm, v_hbm, count_ref, trim_ref, rows_ref, wg_hbm, wu_hbm, wd_hbm,
    attn_ref, ffn_ref,
    q, k, v, wg, wu, wd,
    xp, xmat, psend, xr, ztotal, zsend, zr, hall, down, ysend, yr, fsend, fr, asend, ax, ar,
    load_sem, x_s, x_r, c_s, c_r, px_s, px_r, pz_s, pz_r, hz_s, hz_r, hx_s, hx_r, hd_s, hd_r, y_s, y_r, f_s, f_r, a_s, a_r,
):
    x = lax.axis_index("dom")
    tp = lax.axis_index("tp")
    z = lax.axis_index("dp")
    core = lax.rem(tp, 2)
    y = lax.rem(tp // 2, 8)
    h = tp // 16

    def plane(i, j):
        return (lax.rem(x + i, 4), tp, lax.rem(z + j, 4))

    def chip(i, j):
        return (x, lax.rem(h + i, 2) * 16 + lax.rem(y + j, 8) * 2 + core, z)

    sibling = (x, tp + 1 - 2 * core, z)

    def send(src, dst, ss, rs, to):
        cp = pltpu.make_async_remote_copy(
            src_ref=src, dst_ref=dst, send_sem=ss, recv_sem=rs, device_id=to, device_id_type=MESH
        )
        cp.start()
        return cp

    def arrived(ref, sem):
        pltpu.make_async_copy(ref, ref, sem).wait()

    barrier = pltpu.get_barrier_semaphore()
    partners = (
        [chip(0, j) for j in range(1, 8)] + [chip(1, 0), sibling]
        + [plane(i, 0) for i in (1, 2, 3)] + [plane(0, j) for j in (1, 2, 3)]
    )
    for to in partners:
        pl.semaphore_signal(barrier, inc=1, device_id=to, device_id_type=MESH)
    loads = [
        pltpu.make_async_copy(src, dst, load_sem.at[n])
        for n, (src, dst) in enumerate(
            [(q_hbm.at[0], q), (k_hbm.at[0], k), (v_hbm.at[0], v), (wg_hbm, wg), (wu_hbm, wu), (wd_hbm, wd)]
        )
    ]
    for cp in loads:
        cp.start()
    xp[0, 0, 0] = fold(rows_ref[...].astype(F32)).astype(BF16)

    p = x * 4 + z
    sub, lane = iota((16, 16), 0), iota((16, 16), 1)
    counts = jnp.broadcast_to(count_ref[...].astype(F32), (16, 16))
    count_col = jnp.sum(jnp.where(lane == sub, counts, 0.0), axis=1, keepdims=True)
    start_lane = jnp.sum(jnp.where(sub < lane, count_col, 0.0), axis=0, keepdims=True)
    end_lane = jnp.sum(jnp.where(sub <= lane, count_col, 0.0), axis=0, keepdims=True)
    start_col = jnp.sum(jnp.where(lane < sub, counts, 0.0), axis=1, keepdims=True)
    end_col = start_col + count_col
    block = (p * 4 + (iota((8, 16), 0) & 3)).astype(F32)
    mine = jnp.logical_and(start_lane <= block, block < end_lane)
    trim_of = jnp.sum(jnp.where(mine, trim_ref[...].astype(F32), 0.0), axis=1, keepdims=True)
    end_of = jnp.sum(jnp.where(mine, end_lane, 0.0), axis=1, keepdims=True)
    limit = jnp.where(block[:, :1] == end_of - 1.0, 128.0 - trim_of, 128.0)
    pos = iota((8, 512), 1)
    live = jnp.logical_and(pos // 128 == (iota((8, 512), 0) & 3), (pos & 127).astype(F32) < limit)
    bias8 = jnp.where(live, 0.0, NEG)
    bias = jnp.concatenate([bias8] * 8, axis=0)
    onehot = jnp.where(mine, 1.0, 0.0).astype(BF16)
    is_slot = (iota((64, 128), 0) & 7) < 4
    stat_lane = iota((64, 128), 1)

    for cp in loads[:3]:
        cp.wait()
    def attend(first, last):
        for n in range(first, last):
            chosen = jnp.dot(onehot, q[:, n * 1024 : (n + 1) * 1024], preferred_element_type=F32)
            query = jnp.concatenate([chosen[:, j * 128 : (j + 1) * 128] for j in range(8)], axis=0).astype(BF16)
            scores = lax.dot_general(
                query, k[:, n * 128 : (n + 1) * 128], (((1,), (1,)), ((), ())), preferred_element_type=F32
            ) * (HEAD_SIZE ** -0.5) + bias
            top = jnp.max(scores, axis=1, keepdims=True).astype(BF16).astype(F32)
            weights = jnp.exp(scores - top).astype(BF16)
            total = jnp.sum(weights.astype(F32), axis=1, keepdims=True)
            total_hi = total.astype(BF16).astype(F32)
            numer = jnp.dot(weights, v[:, n * 128 : (n + 1) * 128], preferred_element_type=F32)
            stat = jnp.where(stat_lane < 32, top, jnp.where(stat_lane < 64, total_hi, total - total_hi))
            tile = jnp.where(is_slot, numer, stat).astype(BF16)
            asend[n // 2, n % 2 * 2] = tile[:32]
            asend[n // 2, n % 2 * 2 + 1] = tile[32:]

    attend(0, 2)
    pl.semaphore_wait(barrier, len(partners))

    xs = {}
    xs[1, 0] = send(xp.at[0, 0, 0], xp.at[1, 0, 0], x_s.at[1, 0], x_r.at[1, 0], chip(1, 0))
    for j in (4, 3, 5, 2, 6, 1, 7):
        xs[0, j] = send(xp.at[0, 0, 0], xp.at[0, 0, j], x_s.at[0, j], x_r.at[0, j], chip(0, j))

    attend(2, 8)

    def put(n, first, last):
        half, pieces = PARTS[n]
        for e in range(first, last, 2):
            a, b = xp[(half, *pieces[e])].astype(F32), xp[(half, *pieces[e + 1])].astype(F32)
            xmat[n, e * 8 : e * 8 + 16, :256] = jnp.concatenate([a[:8], b[:8]], axis=0).astype(BF16)
            xmat[n, e * 8 : e * 8 + 16, 256:] = jnp.concatenate([a[8:], b[8:]], axis=0).astype(BF16)

    def to_other_core(half):
        return send(xp.at[half, 0], xp.at[half, 1], c_s.at[half], c_r.at[half], sibling)

    def gate_up(n):
        rows = xmat[n]
        for lo, hi in ((0, 256), (256, 512), (512, 768), (768, 896)):
            g = jnp.dot(rows, wg[:, lo:hi], preferred_element_type=F32)
            u = jnp.dot(rows, wu[:, lo:hi], preferred_element_type=F32)
            both = jnp.concatenate([g.reshape(8, 8, hi - lo), u.reshape(8, 8, hi - lo)], axis=1)
            psend[n, :, :, :, lo:hi] = both.astype(BF16).reshape(4, 2, 16, hi - lo)
        return [
            send(psend.at[n, lax.rem(x + i, 4)], xr.at[n, i], px_s.at[n, i], px_r.at[n, i], plane(i, 0))
            for i in (2, 1, 3)
        ]

    def over_x(n, copies):
        for cp in copies:
            cp.wait()
        for r in range(2):
            value = psend[n, x, r].astype(F32)
            for i in (1, 2, 3):
                value = value + xr[n, i, r].astype(F32)
            ztotal[n, 2 * r] = value[:, :512]
            ztotal[n, 2 * r + 1, :, :384] = value[:, 512:]
            ztotal[n, 2 * r + 1, :, 384:] = jnp.zeros((16, 128), F32)
            zsend[n, 2 * r] = value[:, :512].astype(BF16)
            zsend[n, 2 * r + 1, :, :384] = value[:, 512:].astype(BF16)
            zsend[n, 2 * r + 1, :, 384:] = jnp.zeros((16, 128), BF16)
        return [
            send(zsend.at[n, lax.rem(z + j, 4)], zr.at[n, j], pz_s.at[n, j], pz_r.at[n, j], plane(0, j))
            for j in (2, 1, 3)
        ]

    def over_z(n, copies):
        for cp in copies:
            cp.wait()
        value = ztotal[n, z]
        for j in (1, 2, 3):
            value = value + zr[n, j].astype(F32)
        gate, up = value[:8], value[8:]
        hall[n, x, z] = fold(gate / (1.0 + jnp.exp(-gate)) * up).astype(BF16)
        if n in DIRECT:
            return [
                send(hall.at[n, x, z], hall.at[n, x, z], hd_s.at[n, i * 4 + j], hd_r.at[n, i * 4 + j], plane(i, j))
                for i, j in FAR_FIRST
            ]
        return [
            send(hall.at[n, x, z], hall.at[n, x, z], hz_s.at[n, j], hz_r.at[n, j], plane(0, j))
            for j in (2, 1, 3)
        ]

    def gather_z(n, copies):
        if n in DIRECT:
            return copies
        for cp in copies:
            cp.wait_send()
        for j in (1, 2, 3):
            arrived(hall.at[n, x, lax.rem(z + 4 - j, 4)], hz_r.at[n, j])
        return [
            send(hall.at[n, x], hall.at[n, x], hx_s.at[n, i], hx_r.at[n, i], plane(i, 0)) for i in (2, 1, 3)
        ]

    def gather_x(n, copies):
        for cp in copies:
            cp.wait_send()
        if n in DIRECT:
            for i, j in FAR_FIRST:
                arrived(hall.at[n, lax.rem(x + 4 - i, 4), lax.rem(z + 4 - j, 4)], hd_r.at[n, i * 4 + j])
        else:
            for i in (1, 2, 3):
                arrived(hall.at[n, lax.rem(x + 4 - i, 4)], hx_r.at[n, i])
        rows = hall[n].astype(F32).reshape(8, 2, 2, 8, 256)
        out = 0.0
        for i, lo, hi in ((0, 0, 256), (1, 256, 512), (2, 512, 768), (3, 768, 896)):
            part = rows[:, i // 2, i % 2].reshape(64, 256).astype(BF16)[:, : hi - lo]
            out = out + jnp.dot(part, wd[lo:hi, :], preferred_element_type=F32)
        return out

    def other_core(at, rows):
        refs = [r.at[at // 2, pl.ds(at % 2 * 32, rows.shape[0])] for r in (ysend, yr)]
        refs[0][...] = rows.astype(BF16)
        return send(*refs, y_s.at[at], y_r.at[at], sibling)

    kept = {}

    def owners(half, at, rows, order, copy):
        copy.wait()
        rows = rows + yr[half, at : at + rows.shape[0]].astype(F32)
        out = []
        for t, j in order:
            piece = fold(rows[t * 8 : t * 8 + 8])
            if half == 0 and j == 0:
                kept["own"] = piece
                continue
            fsend[half, j] = piece.astype(BF16)
            out.append(
                send(fsend.at[half, j], fr.at[half, j], f_s.at[half, j], f_r.at[half, j], chip(2 - half, 8 - j))
            )
        return out


    sends_ax = [
        send(asend.at[lax.rem(x + i, 4)], ax.at[i], a_s.at[i], a_r.at[i], plane(i, 0)) for i in (2, 1, 3)
    ]
    ax[0] = asend[x]
    xs[1, 0].wait()
    for j in (4, 3, 5, 2, 6, 1, 7):
        xs[1, j] = send(xp.at[1, 0, 0], xp.at[1, 0, j], x_s.at[1, j], x_r.at[1, j], chip(0, j))
    for j in range(1, 8):
        xs[0, j].wait()
    cores_a = to_other_core(0)
    put(0, 0, 8)
    loads[3].wait()
    loads[4].wait()
    px = {0: gate_up(0)}
    cores_a.wait()
    put(1, 0, 8)
    px[1] = gate_up(1)
    for cp in sends_ax:
        cp.wait()
    sends_az = [
        send(ax.at[:, lax.rem(z + j, 4)], ar.at[:, j], a_s.at[4 + j], a_r.at[4 + j], plane(0, j))
        for j in (2, 1, 3)
    ]
    ar[:, 0] = ax[:, z]
    for j in range(1, 8):
        xs[1, j].wait()
    cores_b = to_other_core(1)
    put(2, 0, 4)
    put(3, 0, 4)
    cores_b.wait()
    put(2, 4, 8)
    px[2] = gate_up(2)
    put(3, 4, 8)
    px[3] = gate_up(3)
    pz = {0: over_x(0, px[0])}
    pz[1] = over_x(1, px[1])
    hz = {0: over_z(0, pz[0])}
    pz[2] = over_x(2, px[2])
    hz[1] = over_z(1, pz[1])
    hx = {0: gather_z(0, hz[0])}
    pz[3] = over_x(3, px[3])
    hz[2] = over_z(2, pz[2])
    hx[1] = gather_z(1, hz[1])
    hz[3] = over_z(3, pz[3])
    hx[2] = gather_z(2, hz[2])
    loads[5].wait()
    down[...] = gather_x(0, hx[0])
    core_a = other_core(0, gather_x(1, hx[1]))
    hx[3] = gather_z(3, hz[3])
    sends_f = owners(0, 0, down[...], [(j, j) for j in (4, 3, 5, 2, 6, 1, 7, 0)], core_a)
    rows_far = gather_x(2, hx[2])
    core_far = other_core(2, rows_far[32:])
    sends_f = sends_f + owners(1, 0, rows_far[:32], list(enumerate(FAR)), core_far)
    rows_near = gather_x(3, hx[3])
    core_near = other_core(3, rows_near[32:])
    sends_f = sends_f + owners(1, 32, rows_near[:32], list(enumerate(NEAR)), core_near)
    for cp in sends_az:
        cp.wait()
    col = iota((16, 128), 1)
    from_block = ((((x + 4 - col // 32) & 3) * 4 + ((z + 4 - (col // 8 & 3)) & 3)) * 4 + (col & 3)).astype(F32)
    owns = jnp.logical_and(jnp.logical_and(start_col <= from_block, from_block < end_col), (col & 7) >= 4)
    gathered = ar[...].astype(F32).reshape(16, 32, 128)
    for j in range(4):
        part = gathered[:, j * 8 : (j + 1) * 8, :].reshape(128, 128)
        turned = part.T
        tops, totals = turned[0:1], turned[32:33] + turned[64:65]
        top = jnp.max(jnp.where(owns, tops, NEG), axis=1, keepdims=True)
        scale = jnp.exp(jnp.where(owns, tops - top, NEG))
        den = jnp.sum(scale * totals, axis=1, keepdims=True)
        num = jnp.dot(
            pltpu.roll(scale, 124, 1), part, precision=lax.Precision.HIGHEST, preferred_element_type=F32
        )
        attn_ref[0, :, j * 128 : (j + 1) * 128] = (num / den).astype(BF16)

    piece = kept["own"]
    for i in range(2):
        for cp in sends_f[7 * i : 7 + 8 * i]:
            cp.wait()
        for j in range(1 - i, 8):
            piece = piece + fr[i, j].astype(F32)
    ffn_ref[...] = unfold(piece).astype(BF16)


def shards(query, key_block_pool, value_block_pool, row_blocks, trim, ffn_in, w_gate, w_up, w_down):
    any_ = pl.BlockSpec(memory_space=pl.ANY)
    vmem = pl.BlockSpec(memory_space=pltpu.VMEM)
    dma = pltpu.SemaphoreType.DMA
    return pl.pallas_call(
        kernel,
        out_shape=(pltpu.VMEM((1, 16, 512), BF16), pltpu.VMEM((8, 512), BF16)),
        in_specs=[any_, any_, any_, vmem, vmem, vmem, any_, any_, any_],
        out_specs=(vmem, vmem),
        scratch_shapes=[
            pltpu.VMEM((16, 8192), BF16),
            pltpu.VMEM((512, 1024), BF16),
            pltpu.VMEM((512, 1024), BF16),
            pltpu.VMEM((512, 896), BF16),
            pltpu.VMEM((512, 896), BF16),
            pltpu.VMEM((896, 512), BF16),
            pltpu.VMEM((2, 2, 8, 16, 256), BF16),
            pltpu.VMEM((4, 64, 512), BF16),
            pltpu.VMEM((4, 4, 2, 16, 896), BF16),
            pltpu.VMEM((4, 4, 2, 16, 896), BF16),
            pltpu.VMEM((4, 4, 16, 512), F32),
            pltpu.VMEM((4, 4, 16, 512), BF16),
            pltpu.VMEM((4, 4, 16, 512), BF16),
            pltpu.VMEM((4, 4, 4, 16, 256), BF16),
            pltpu.VMEM((64, 512), F32),
            pltpu.VMEM((2, 64, 512), BF16),
            pltpu.VMEM((2, 64, 512), BF16),
            pltpu.VMEM((2, 8, 16, 256), BF16),
            pltpu.VMEM((2, 8, 16, 256), BF16),
            pltpu.VMEM((4, 4, 32, 128), BF16),
            pltpu.VMEM((4, 4, 32, 128), BF16),
            pltpu.VMEM((4, 4, 32, 128), BF16),
            dma((6,)),
            dma((2, 8)), dma((2, 8)),
            dma((2,)), dma((2,)),
            dma((4, 4)), dma((4, 4)),
            dma((4, 4)), dma((4, 4)),
            dma((4, 4)), dma((4, 4)),
            dma((4, 4)), dma((4, 4)),
            dma((4, 16)), dma((4, 16)),
            dma((4,)), dma((4,)),
            dma((2, 8)), dma((2, 8)),
            dma((8,)), dma((8,)),
        ],
        compiler_params=pltpu.CompilerParams(
            collective_id=0, has_side_effects=True, vmem_limit_bytes=60 << 20
        ),
        name="decode_step",
    )(query, key_block_pool, value_block_pool, row_blocks, trim, ffn_in, w_gate, w_up, w_down)


def solution(mesh):
    in_specs = (
        P("tp", None, None),
        P("tp", ("dom", "dp"), None),
        P("tp", ("dom", "dp"), None),
        P("tp", None),
        P("tp", None),
        P("tp", ("dom", "dp")),
        P(("dom", "dp"), "tp"),
        P(("dom", "dp"), "tp"),
        P("tp", ("dom", "dp")),
    )
    out_specs = (P("tp", None, ("dom", "dp")), P("tp", ("dom", "dp")))
    return jax.shard_map(shards, mesh=mesh, in_specs=in_specs, out_specs=out_specs, check_vma=False)
```

```python
import jax
import jax.numpy as jnp
from jax import lax
from jax.experimental import pallas as pl
from jax.experimental.pallas import tpu as pltpu
from jax.sharding import PartitionSpec as P

QUERY_HEADS = 64
KEY_HEADS = 8
HEAD_SIZE = 128
NEG = -1e30
MESH = pl.DeviceIdType.MESH
F32 = jnp.float32
BF16 = jnp.bfloat16

PLANE = [(i, j) for i in range(4) for j in range(4) if i or j]
CHIPS = [(i, j) for i in range(2) for j in range(8) if i or j]

FAR_FIRST = sorted(PLANE, key=lambda t: -(min(t[0], 4 - t[0]) + min(t[1], 4 - t[1])))
DIRECT = (2, 3,)
FAR, NEAR = (4, 3, 5, 2), (6, 1, 7, 0)
PARTS = (
    (0, [(0, j) for j in range(8)]),
    (0, [(1, j) for j in range(8)]),
    (1, [(c, j) for c in (0, 1) for j in FAR]),
    (1, [(c, j) for c in (0, 1) for j in NEAR]),
)


def iota(shape, axis):
    return lax.broadcasted_iota(jnp.int32, shape, axis)


def fold(rows):
    return jnp.concatenate([rows[:, :256], rows[:, 256:]], axis=0)


def unfold(piece):
    return jnp.concatenate([piece[:8], piece[8:]], axis=1)


def kernel(
    q_hbm, k_hbm, v_hbm, count_ref, trim_ref, rows_ref, wg_hbm, wu_hbm, wd_hbm,
    attn_ref, ffn_ref,
    q, k, v, wg, wu, wd,
    xp, xmat, psend, xr, ztotal, zsend, zr, hall, down, ysend, yr, fsend, fr, asend, ax, ar,
    load_sem, x_s, x_r, c_s, c_r, px_s, px_r, pz_s, pz_r, hz_s, hz_r, hx_s, hx_r, hd_s, hd_r, y_s, y_r, f_s, f_r, a_s, a_r,
):
    x = lax.axis_index("dom")
    tp = lax.axis_index("tp")
    z = lax.axis_index("dp")
    core = lax.rem(tp, 2)
    y = lax.rem(tp // 2, 8)
    h = tp // 16

    def plane(i, j):
        return (lax.rem(x + i, 4), tp, lax.rem(z + j, 4))

    def chip(i, j):
        return (x, lax.rem(h + i, 2) * 16 + lax.rem(y + j, 8) * 2 + core, z)

    sibling = (x, tp + 1 - 2 * core, z)

    def send(src, dst, ss, rs, to):
        cp = pltpu.make_async_remote_copy(
            src_ref=src, dst_ref=dst, send_sem=ss, recv_sem=rs, device_id=to, device_id_type=MESH
        )
        cp.start()
        return cp

    def arrived(ref, sem):
        pltpu.make_async_copy(ref, ref, sem).wait()

    barrier = pltpu.get_barrier_semaphore()
    partners = (
        [chip(0, 4), chip(1, 0)] + [chip(0, j) for j in (3, 5, 2, 6, 1, 7)] + [sibling]
        + [plane(i, 0) for i in (1, 2, 3)] + [plane(0, j) for j in (1, 2, 3)]
    )
    for to in partners:
        pl.semaphore_signal(barrier, inc=1, device_id=to, device_id_type=MESH)
    loads = [
        pltpu.make_async_copy(src, dst, load_sem.at[n])
        for n, (src, dst) in enumerate(
            [(q_hbm.at[0], q), (k_hbm.at[0], k), (v_hbm.at[0], v), (wg_hbm, wg), (wu_hbm, wu), (wd_hbm, wd)]
        )
    ]
    for cp in loads:
        cp.start()
    xp[0, 0, 0] = fold(rows_ref[...].astype(F32)).astype(BF16)

    p = x * 4 + z
    sub, lane = iota((16, 16), 0), iota((16, 16), 1)
    counts = jnp.broadcast_to(count_ref[...].astype(F32), (16, 16))
    count_col = jnp.sum(jnp.where(lane == sub, counts, 0.0), axis=1, keepdims=True)
    start_lane = jnp.sum(jnp.where(sub < lane, count_col, 0.0), axis=0, keepdims=True)
    end_lane = jnp.sum(jnp.where(sub <= lane, count_col, 0.0), axis=0, keepdims=True)
    start_col = jnp.sum(jnp.where(lane < sub, counts, 0.0), axis=1, keepdims=True)
    end_col = start_col + count_col
    block = (p * 4 + (iota((8, 16), 0) & 3)).astype(F32)
    mine = jnp.logical_and(start_lane <= block, block < end_lane)
    trim_of = jnp.sum(jnp.where(mine, trim_ref[...].astype(F32), 0.0), axis=1, keepdims=True)
    end_of = jnp.sum(jnp.where(mine, end_lane, 0.0), axis=1, keepdims=True)
    limit = jnp.where(block[:, :1] == end_of - 1.0, 128.0 - trim_of, 128.0)
    pos = iota((8, 512), 1)
    live = jnp.logical_and(pos // 128 == (iota((8, 512), 0) & 3), (pos & 127).astype(F32) < limit)
    bias8 = jnp.where(live, 0.0, NEG)
    bias = jnp.concatenate([bias8] * 8, axis=0)
    onehot = jnp.where(mine, 1.0, 0.0).astype(BF16)
    is_slot = (iota((64, 128), 0) & 7) < 4
    stat_lane = iota((64, 128), 1)

    for cp in loads[:3]:
        cp.wait()
    def attend(first, last):
        for n in range(first, last):
            chosen = jnp.dot(onehot, q[:, n * 1024 : (n + 1) * 1024], preferred_element_type=F32)
            query = jnp.concatenate([chosen[:, j * 128 : (j + 1) * 128] for j in range(8)], axis=0).astype(BF16)
            scores = lax.dot_general(
                query, k[:, n * 128 : (n + 1) * 128], (((1,), (1,)), ((), ())), preferred_element_type=F32
            ) * (HEAD_SIZE ** -0.5) + bias
            top = jnp.max(scores, axis=1, keepdims=True).astype(BF16).astype(F32)
            weights = jnp.exp(scores - top).astype(BF16)
            total = jnp.sum(weights.astype(F32), axis=1, keepdims=True)
            total_hi = total.astype(BF16).astype(F32)
            numer = jnp.dot(weights, v[:, n * 128 : (n + 1) * 128], preferred_element_type=F32)
            stat = jnp.where(stat_lane < 32, top, jnp.where(stat_lane < 64, total_hi, total - total_hi))
            tile = jnp.where(is_slot, numer, stat).astype(BF16)
            asend[n // 2, n % 2 * 2] = tile[:32]
            asend[n // 2, n % 2 * 2 + 1] = tile[32:]

    attend(0, 2)
    pl.semaphore_wait(barrier, len(partners))

    xs = {}
    xs[1, 0] = send(xp.at[0, 0, 0], xp.at[1, 0, 0], x_s.at[1, 0], x_r.at[1, 0], chip(1, 0))
    for j in (4, 3, 5, 2, 6, 1, 7):
        xs[0, j] = send(xp.at[0, 0, 0], xp.at[0, 0, j], x_s.at[0, j], x_r.at[0, j], chip(0, j))

    attend(2, 8)

    def put(n, first, last):
        half, pieces = PARTS[n]
        for e in range(first, last, 2):
            a, b = xp[(half, *pieces[e])].astype(F32), xp[(half, *pieces[e + 1])].astype(F32)
            xmat[n, e * 8 : e * 8 + 16, :256] = jnp.concatenate([a[:8], b[:8]], axis=0).astype(BF16)
            xmat[n, e * 8 : e * 8 + 16, 256:] = jnp.concatenate([a[8:], b[8:]], axis=0).astype(BF16)

    def to_other_core(half):
        return send(xp.at[half, 0], xp.at[half, 1], c_s.at[half], c_r.at[half], sibling)

    def gate_up(n):
        rows = xmat[n]
        for lo, hi in ((0, 256), (256, 512), (512, 768), (768, 896)):
            g = jnp.dot(rows, wg[:, lo:hi], preferred_element_type=F32)
            u = jnp.dot(rows, wu[:, lo:hi], preferred_element_type=F32)
            both = jnp.concatenate([g.reshape(8, 8, hi - lo), u.reshape(8, 8, hi - lo)], axis=1)
            psend[n, :, :, :, lo:hi] = both.astype(BF16).reshape(4, 2, 16, hi - lo)
        return [
            send(psend.at[n, lax.rem(x + i, 4)], xr.at[n, i], px_s.at[n, i], px_r.at[n, i], plane(i, 0))
            for i in (2, 1, 3)
        ]

    def over_x(n, copies):
        for cp in copies:
            cp.wait()
        for r in range(2):
            value = psend[n, x, r].astype(F32)
            for i in (1, 2, 3):
                value = value + xr[n, i, r].astype(F32)
            ztotal[n, 2 * r] = value[:, :512]
            ztotal[n, 2 * r + 1, :, :384] = value[:, 512:]
            ztotal[n, 2 * r + 1, :, 384:] = jnp.zeros((16, 128), F32)
            zsend[n, 2 * r] = value[:, :512].astype(BF16)
            zsend[n, 2 * r + 1, :, :384] = value[:, 512:].astype(BF16)
            zsend[n, 2 * r + 1, :, 384:] = jnp.zeros((16, 128), BF16)
        return [
            send(zsend.at[n, lax.rem(z + j, 4)], zr.at[n, j], pz_s.at[n, j], pz_r.at[n, j], plane(0, j))
            for j in (2, 1, 3)
        ]

    def over_z(n, copies):
        for cp in copies:
            cp.wait()
        value = ztotal[n, z]
        for j in (1, 2, 3):
            value = value + zr[n, j].astype(F32)
        gate, up = value[:8], value[8:]
        hall[n, x, z] = fold(gate / (1.0 + jnp.exp(-gate)) * up).astype(BF16)
        if n in DIRECT:
            return [
                send(hall.at[n, x, z], hall.at[n, x, z], hd_s.at[n, i * 4 + j], hd_r.at[n, i * 4 + j], plane(i, j))
                for i, j in FAR_FIRST
            ]
        return [
            send(hall.at[n, x, z], hall.at[n, x, z], hz_s.at[n, j], hz_r.at[n, j], plane(0, j))
            for j in (2, 1, 3)
        ]

    def gather_z(n, copies):
        if n in DIRECT:
            return copies
        for cp in copies:
            cp.wait_send()
        for j in (1, 2, 3):
            arrived(hall.at[n, x, lax.rem(z + 4 - j, 4)], hz_r.at[n, j])
        return [
            send(hall.at[n, x], hall.at[n, x], hx_s.at[n, i], hx_r.at[n, i], plane(i, 0)) for i in (2, 1, 3)
        ]

    def gather_x(n, copies):
        for cp in copies:
            cp.wait_send()
        if n in DIRECT:
            for i, j in FAR_FIRST:
                arrived(hall.at[n, lax.rem(x + 4 - i, 4), lax.rem(z + 4 - j, 4)], hd_r.at[n, i * 4 + j])
        else:
            for i in (1, 2, 3):
                arrived(hall.at[n, lax.rem(x + 4 - i, 4)], hx_r.at[n, i])
        rows = hall[n].astype(F32).reshape(8, 2, 2, 8, 256)
        out = 0.0
        for i, lo, hi in ((0, 0, 256), (1, 256, 512), (2, 512, 768), (3, 768, 896)):
            part = rows[:, i // 2, i % 2].reshape(64, 256).astype(BF16)[:, : hi - lo]
            out = out + jnp.dot(part, wd[lo:hi, :], preferred_element_type=F32)
        return out

    def other_core(at, rows):
        refs = [r.at[at // 2, pl.ds(at % 2 * 32, rows.shape[0])] for r in (ysend, yr)]
        refs[0][...] = rows.astype(BF16)
        return send(*refs, y_s.at[at], y_r.at[at], sibling)

    kept = {}

    def owners(half, at, rows, order, copy):
        copy.wait()
        rows = rows + yr[half, at : at + rows.shape[0]].astype(F32)
        out = []
        for t, j in order:
            piece = fold(rows[t * 8 : t * 8 + 8])
            if half == 0 and j == 0:
                kept["own"] = piece
                continue
            fsend[half, j] = piece.astype(BF16)
            out.append(
                send(fsend.at[half, j], fr.at[half, j], f_s.at[half, j], f_r.at[half, j], chip(2 - half, 8 - j))
            )
        return out


    sends_ax = [
        send(asend.at[lax.rem(x + i, 4)], ax.at[i], a_s.at[i], a_r.at[i], plane(i, 0)) for i in (2, 1, 3)
    ]
    ax[0] = asend[x]
    xs[1, 0].wait()
    for j in (4, 3, 5, 2, 6, 1, 7):
        xs[1, j] = send(xp.at[1, 0, 0], xp.at[1, 0, j], x_s.at[1, j], x_r.at[1, j], chip(0, j))
    for j in range(1, 8):
        xs[0, j].wait()
    cores_a = to_other_core(0)
    put(0, 0, 8)
    loads[3].wait()
    loads[4].wait()
    px = {0: gate_up(0)}
    cores_a.wait()
    put(1, 0, 8)
    px[1] = gate_up(1)
    for cp in sends_ax:
        cp.wait()
    sends_az = [
        send(ax.at[:, lax.rem(z + j, 4)], ar.at[:, j], a_s.at[4 + j], a_r.at[4 + j], plane(0, j))
        for j in (2, 1, 3)
    ]
    ar[:, 0] = ax[:, z]
    for j in range(1, 8):
        xs[1, j].wait()
    cores_b = to_other_core(1)
    put(2, 0, 4)
    put(3, 0, 4)
    cores_b.wait()
    put(2, 4, 8)
    px[2] = gate_up(2)
    put(3, 4, 8)
    px[3] = gate_up(3)
    pz = {0: over_x(0, px[0])}
    pz[1] = over_x(1, px[1])
    hz = {0: over_z(0, pz[0])}
    pz[2] = over_x(2, px[2])
    hz[1] = over_z(1, pz[1])
    pz[3] = over_x(3, px[3])
    hx = {0: gather_z(0, hz[0])}
    hz[2] = over_z(2, pz[2])
    hx[1] = gather_z(1, hz[1])
    hz[3] = over_z(3, pz[3])
    hx[2] = gather_z(2, hz[2])
    loads[5].wait()
    down[...] = gather_x(0, hx[0])
    core_a = other_core(0, gather_x(1, hx[1]))
    hx[3] = gather_z(3, hz[3])
    sends_f = owners(0, 0, down[...], [(j, j) for j in (4, 3, 5, 2, 6, 1, 7, 0)], core_a)
    rows_far = gather_x(2, hx[2])
    core_far = other_core(2, rows_far[32:])
    sends_f = sends_f + owners(1, 0, rows_far[:32], list(enumerate(FAR)), core_far)
    rows_near = gather_x(3, hx[3])
    core_near = other_core(3, rows_near[32:])
    sends_f = sends_f + owners(1, 32, rows_near[:32], list(enumerate(NEAR)), core_near)
    for cp in sends_az:
        cp.wait()
    col = iota((16, 128), 1)
    from_block = ((((x + 4 - col // 32) & 3) * 4 + ((z + 4 - (col // 8 & 3)) & 3)) * 4 + (col & 3)).astype(F32)
    owns = jnp.logical_and(jnp.logical_and(start_col <= from_block, from_block < end_col), (col & 7) >= 4)
    gathered = ar[...].astype(F32).reshape(16, 32, 128)
    for j in range(4):
        part = gathered[:, j * 8 : (j + 1) * 8, :].reshape(128, 128)
        turned = part.T
        tops, totals = turned[0:1], turned[32:33] + turned[64:65]
        top = jnp.max(jnp.where(owns, tops, NEG), axis=1, keepdims=True)
        scale = jnp.exp(jnp.where(owns, tops - top, NEG))
        den = jnp.sum(scale * totals, axis=1, keepdims=True)
        num = jnp.dot(
            pltpu.roll(scale, 124, 1), part, precision=lax.Precision.HIGHEST, preferred_element_type=F32
        )
        attn_ref[0, :, j * 128 : (j + 1) * 128] = (num / den).astype(BF16)

    piece = kept["own"]
    for i in range(2):
        for cp in sends_f[7 * i : 7 + 8 * i]:
            cp.wait()
        for j in range(1 - i, 8):
            piece = piece + fr[i, j].astype(F32)
    ffn_ref[...] = unfold(piece).astype(BF16)


def shards(query, key_block_pool, value_block_pool, row_blocks, trim, ffn_in, w_gate, w_up, w_down):
    any_ = pl.BlockSpec(memory_space=pl.ANY)
    vmem = pl.BlockSpec(memory_space=pltpu.VMEM)
    dma = pltpu.SemaphoreType.DMA
    return pl.pallas_call(
        kernel,
        out_shape=(pltpu.VMEM((1, 16, 512), BF16), pltpu.VMEM((8, 512), BF16)),
        in_specs=[any_, any_, any_, vmem, vmem, vmem, any_, any_, any_],
        out_specs=(vmem, vmem),
        scratch_shapes=[
            pltpu.VMEM((16, 8192), BF16),
            pltpu.VMEM((512, 1024), BF16),
            pltpu.VMEM((512, 1024), BF16),
            pltpu.VMEM((512, 896), BF16),
            pltpu.VMEM((512, 896), BF16),
            pltpu.VMEM((896, 512), BF16),
            pltpu.VMEM((2, 2, 8, 16, 256), BF16),
            pltpu.VMEM((4, 64, 512), BF16),
            pltpu.VMEM((4, 4, 2, 16, 896), BF16),
            pltpu.VMEM((4, 4, 2, 16, 896), BF16),
            pltpu.VMEM((4, 4, 16, 512), F32),
            pltpu.VMEM((4, 4, 16, 512), BF16),
            pltpu.VMEM((4, 4, 16, 512), BF16),
            pltpu.VMEM((4, 4, 4, 16, 256), BF16),
            pltpu.VMEM((64, 512), F32),
            pltpu.VMEM((2, 64, 512), BF16),
            pltpu.VMEM((2, 64, 512), BF16),
            pltpu.VMEM((2, 8, 16, 256), BF16),
            pltpu.VMEM((2, 8, 16, 256), BF16),
            pltpu.VMEM((4, 4, 32, 128), BF16),
            pltpu.VMEM((4, 4, 32, 128), BF16),
            pltpu.VMEM((4, 4, 32, 128), BF16),
            dma((6,)),
            dma((2, 8)), dma((2, 8)),
            dma((2,)), dma((2,)),
            dma((4, 4)), dma((4, 4)),
            dma((4, 4)), dma((4, 4)),
            dma((4, 4)), dma((4, 4)),
            dma((4, 4)), dma((4, 4)),
            dma((4, 16)), dma((4, 16)),
            dma((4,)), dma((4,)),
            dma((2, 8)), dma((2, 8)),
            dma((8,)), dma((8,)),
        ],
        compiler_params=pltpu.CompilerParams(
            collective_id=0, has_side_effects=True, vmem_limit_bytes=60 << 20
        ),
        name="decode_step",
    )(query, key_block_pool, value_block_pool, row_blocks, trim, ffn_in, w_gate, w_up, w_down)


def solution(mesh):
    in_specs = (
        P("tp", None, None),
        P("tp", ("dom", "dp"), None),
        P("tp", ("dom", "dp"), None),
        P("tp", None),
        P("tp", None),
        P("tp", ("dom", "dp")),
        P(("dom", "dp"), "tp"),
        P(("dom", "dp"), "tp"),
        P("tp", ("dom", "dp")),
    )
    out_specs = (P("tp", None, ("dom", "dp")), P("tp", ("dom", "dp")))
    return jax.shard_map(shards, mesh=mesh, in_specs=in_specs, out_specs=out_specs, check_vma=False)
```
